768 devices in a mesh: vol: 64 (over x, y, core), seq: 12 (over z).
Axes of the slice: x: 4, y: 8, z: 12, core: 2. Of those that a mesh axis runs over, the one named last changes fastest.
Arguments:
- patches: bfloat16 [64, 3072, 1024], P('vol', 'seq'), may hold values from -6 to 6
- visible: int32 [64, 12, 96], P('vol', 'seq'), may hold values from 0 to 255, as said below
- counts: int32 [64, 12], P('vol'), may hold values from 32 to 96, as said below
- pos_embed: bfloat16 [3072, 512], P('seq'), may hold values from -3 to 3
- mask_token: bfloat16 [512], replicated, may hold values from -4 to 4
- enc_gain: bfloat16 [1024], replicated, may hold values from 0.099609375 to 1.8984375
- enc_qkv: bfloat16 [1024, 2304], P('vol')
- enc_wo: bfloat16 [768, 1024], replicated, may hold values from -1.75 to 1.75
- enc_to_dec: bfloat16 [1024, 512], replicated, may hold values from -0.1875 to 0.1875
- dec_gain: bfloat16 [512], replicated, may hold values from 0.099609375 to 1.8984375
- dec_qkv: bfloat16 [512, 1536], replicated
- dec_wo: bfloat16 [512, 512], replicated, may hold values from -0.25 to 0.25
Outputs:
- decoded: bfloat16 [64, 3072, 512], P('vol', 'seq')
The draws below stay inside these ranges and needn't reach their ends.
Inputs may be any that keep to these rules, and one draw needn't show every extreme that they name: `counts`: live visible slots of each shard; in every volume some shard has exactly 96. In each shard the first counts entries are the shard's visible token positions in increasing order; the other entries are distinct positions of masked tokens of that shard.
All inputs are finite; a program needn't handle non-finite values.
Results may differ from the reference program's by a relative error of at most 0.014.
Values may be sent and summed in bfloat16 or wider, within the bound.
A program may use at most 64 MiB of HBM per device.

```python
import math
import jax
import jax.numpy as jnp
from jax import lax

D = 1024
HEADS = 12
HD = 64
HA = 768
DD = 512
DHEADS = 16
LAYER = 128
TOK_DEV = 256
CAP = 96
VOLS = 64
NZ = 24
SEQ_TOK = 3072
N_SEQ = 12


def mask_layout(key):
    key_count, key_full, key_order = jax.random.split(key, 3)
    drawn = jax.random.randint(key_count, (VOLS, N_SEQ), TOK_DEV // 8, CAP + 1)
    fullest = jax.random.randint(key_full, (VOLS, 1), 0, N_SEQ)
    shard_counts = jnp.where(jnp.arange(N_SEQ)[None, :] == fullest, CAP, drawn).astype(jnp.int32)
    order_score = jax.random.randint(key_order, (VOLS, N_SEQ, TOK_DEV), 0, 1 << 18) * TOK_DEV + jnp.arange(TOK_DEV)[None, None, :]
    order = jnp.argsort(order_score, axis=-1).astype(jnp.int32)
    rank_index = jnp.arange(TOK_DEV)[None, None, :]
    shifted = jnp.where(rank_index < shard_counts[:, :, None], order, order + TOK_DEV)
    chosen = jnp.sort(shifted, axis=-1)[:, :, :CAP] % TOK_DEV
    return (shard_counts, chosen.astype(jnp.int32))


def draw_visible(key, part):
    return mask_layout(key)[1]


def draw_counts(key, part):
    return mask_layout(key)[0]


def drawn_projection(key, row_count, head_count, head_size, lowest):
    total_width = head_count * head_size
    key_q, key_k, key_v, key_s = jax.random.split(key, 4)
    row_scale = row_count ** (-0.5)
    query_part = jax.random.normal(key_q, (row_count, total_width), jnp.float32) * row_scale
    key_part = jax.random.normal(key_k, (row_count, total_width), jnp.float32) * row_scale
    value_part = jax.random.normal(key_v, (row_count, total_width), jnp.float32) * row_scale
    strength = jnp.exp(jax.random.uniform(key_s, (head_count,), jnp.float32, math.log(lowest), 1e-06))
    strength = jnp.repeat(strength, head_size)[None, :]
    key_part = key_part * strength
    return jnp.concatenate([query_part, key_part, value_part], axis=1)


def draw_enc_qkv(key, part):
    key = jax.random.fold_in(key, 11)
    return drawn_projection(key, D, HEADS, HD, 1.0).astype(jnp.bfloat16)


def draw_dec_qkv(key, part):
    key = jax.random.fold_in(key, 13)
    return drawn_projection(key, DD, DHEADS, DD // DHEADS, 1.0).astype(jnp.bfloat16)


def levels(stream_key, dims, cuts, smallest, largest):
    def one(position, shards_of):
        heights = jax.random.uniform(jax.random.fold_in(jax.random.fold_in(stream_key, 6), position), (shards_of,), jnp.float32, smallest / len(cuts), largest / len(cuts))
        return jnp.repeat(jnp.exp(heights), dims[position] // shards_of).reshape((-1,) + (1,) * (len(dims) - position - 1))

    factor_of = one(*cuts[0])
    for cut in cuts[1:]:
        factor_of = factor_of * one(*cut)
    return factor_of


def gaussian(rng, shape, scale, limit, shards=(), kind=jnp.bfloat16):
    array = scale * jax.random.normal(rng, shape, jnp.float32)
    if shards:
        array = array * levels(rng, shape, shards, -0.22, 0.18)
    return jnp.clip(array, -limit, limit).astype(kind)


def setup_inputs(seed: int = 0) -> dict:
    key_list = jax.random.split(jax.random.key(seed), 13)
    return {
        "patches": gaussian(key_list[0], (VOLS, SEQ_TOK, D), 1.0, 6.0, ((0, 64), (1, 12))),
        "visible": draw_visible(jax.random.fold_in(key_list[12], 71), 0),
        "counts": draw_counts(jax.random.fold_in(key_list[12], 71), 0),
        "pos_embed": gaussian(key_list[3], (SEQ_TOK, DD), 0.5, 3.0, ((0, 12),)),
        "mask_token": gaussian(key_list[4], (DD,), 1.0, 4.0),
        "enc_gain": jnp.clip(1.0 + 0.18 * jax.random.normal(key_list[5], (D,), jnp.float32), 0.099609375, 1.8984375).astype(jnp.bfloat16),
        "enc_qkv": draw_enc_qkv(jax.random.fold_in(key_list[12], 71), 0),
        "enc_wo": gaussian(key_list[7], (HA, D), (HA // 64) ** -0.5, 1.75),
        "enc_to_dec": gaussian(key_list[8], (D, DD), D ** -0.5, 0.1875),
        "dec_gain": jnp.clip(1.0 + 0.18 * jax.random.normal(key_list[9], (DD,), jnp.float32), 0.099609375, 1.8984375).astype(jnp.bfloat16),
        "dec_qkv": draw_dec_qkv(jax.random.fold_in(key_list[12], 71), 0),
        "dec_wo": gaussian(key_list[11], (DD, DD), DD ** -0.5, 0.25),
    }


EPSILON = 1e-06
NEGATIVE = -1e+30

def layer_norm(values, weights):
    values = values.astype(jnp.float32)
    centred = values - lax.optimization_barrier(jnp.mean(values, axis=-1, keepdims=True))
    spread = lax.optimization_barrier(jnp.mean(centred * centred, axis=-1, keepdims=True))
    return centred * lax.rsqrt(spread + EPSILON) * weights.astype(jnp.float32)

def attend(queries, key_rows, values, key_live, head_size):
    scores = jnp.einsum('qhd,khd->hqk', queries.astype(jnp.float32), key_rows.astype(jnp.float32))
    scores = scores * (1.0 / math.sqrt(head_size))
    scores = jnp.where(key_live, scores, NEGATIVE)
    highest = lax.optimization_barrier(jnp.max(scores, axis=-1, keepdims=True))
    raised = jnp.where(key_live, jnp.exp(scores - highest), 0.0)
    denom_sum = lax.optimization_barrier(jnp.sum(raised, axis=-1))
    weights = raised.astype(jnp.bfloat16)
    mixed_rows = jnp.einsum('hqk,khd->qhd', weights.astype(jnp.float32), values.astype(jnp.float32))
    mixed_rows = mixed_rows / jnp.transpose(denom_sum)[:, :, None]
    return mixed_rows.astype(jnp.bfloat16).reshape(queries.shape[0], -1)

def reference(patches, visible, counts, pos_embed, mask_token, enc_gain, enc_qkv, enc_wo, enc_to_dec, dec_gain, dec_qkv, dec_wo):
    dec_head = DD // DHEADS

    def one_volume(inputs):
        patch_rows, vis_rows, count_row = inputs
        shard_base = jnp.arange(N_SEQ, dtype=jnp.int32)[:, None] * TOK_DEV
        slot_token = (vis_rows.astype(jnp.int32) + shard_base).reshape(-1).astype(jnp.int32)
        slot_live = (jnp.arange(CAP, dtype=jnp.int32)[None, :] < count_row[:, None]).reshape(-1)
        x_vis = patch_rows[slot_token]
        enc_norm = layer_norm(x_vis, enc_gain).astype(jnp.bfloat16)
        enc_proj = jnp.dot(enc_norm, enc_qkv, preferred_element_type=jnp.float32).astype(jnp.bfloat16)
        split_heads = enc_proj.reshape(N_SEQ * CAP, 3, HEADS, HD)
        enc_mix = attend(split_heads[:, 0], split_heads[:, 1], split_heads[:, 2], slot_live[None, None, :], HD)
        enc_out = (x_vis.astype(jnp.float32) + jnp.dot(enc_mix, enc_wo, preferred_element_type=jnp.float32)).astype(jnp.bfloat16)
        latent = jnp.dot(enc_out, enc_to_dec, preferred_element_type=jnp.float32).astype(jnp.bfloat16)
        live_float = slot_live.astype(jnp.float32)
        placed = jnp.zeros((SEQ_TOK, DD), jnp.float32).at[slot_token].add(latent.astype(jnp.float32) * live_float[:, None])
        is_visible = jnp.zeros((SEQ_TOK,), jnp.float32).at[slot_token].add(live_float)
        dec_in = jnp.where(is_visible[:, None] > 0.5, placed, mask_token.astype(jnp.float32)[None, :]) + pos_embed.astype(jnp.float32)
        dec_norm = layer_norm(dec_in, dec_gain).astype(jnp.bfloat16)
        dec_proj = jnp.dot(dec_norm, dec_qkv, preferred_element_type=jnp.float32).astype(jnp.bfloat16)
        by_level = dec_proj.reshape(NZ, LAYER, 3 * DD)
        padded = jnp.pad(by_level, ((1, 1), (0, 0), (0, 0)))

        def one_level(z_level):
            window = lax.dynamic_slice_in_dim(padded, z_level, 3, 0).reshape(3 * LAYER, 3, DHEADS, dec_head)
            queries = lax.dynamic_slice_in_dim(by_level, z_level, 1, 0).reshape(LAYER, 3, DHEADS, dec_head)
            global_level = z_level - 1 + jnp.arange(3, dtype=jnp.int32)
            level_live = (global_level >= 0) & (global_level < NZ)
            key_live = jnp.repeat(level_live, LAYER)
            return attend(queries[:, 0], window[:, 1], window[:, 2], key_live[None, None, :], dec_head)
        dec_mix = lax.map(one_level, jnp.arange(NZ, dtype=jnp.int32)).reshape(SEQ_TOK, DD)
        return (dec_in + jnp.dot(dec_mix, dec_wo, preferred_element_type=jnp.float32)).astype(jnp.bfloat16)
    return lax.map(one_volume, (patches, visible, counts))
```

```python
import functools
import math

import jax
import jax.numpy as jnp
from jax import lax
from jax.experimental import pallas as pl
from jax.experimental.pallas import tpu as pltpu
from jax.sharding import PartitionSpec as P

MESH = pl.DeviceIdType.MESH
BF = jnp.bfloat16
F32 = jnp.float32

HEADS = 12
DHEADS = 16
NX, NY, NC, NZ = 4, 8, 2, 12
CAP = 96
TOK = 256
LAYER = 128
D = 1024
HA = 768
HG = HA // 2
WG = 3 * HG
DD = 512
ROWS = 16
HALF = CAP // 2
EPSILON = 1e-06
NEGATIVE = -1e30
OWN = 4
FIRST = 9
LOG2E = math.log2(math.e)


def dot(a, b):
    return jnp.dot(a, b, preferred_element_type=F32)


def dot_nt(a, b):
    return lax.dot_general(a, b, (((1,), (1,)), ((), ())), preferred_element_type=F32)


def layer_norm(values, weights):
    centred = values - jnp.mean(values, axis=-1, keepdims=True)
    spread = jnp.mean(centred * centred, axis=-1, keepdims=True)
    return centred * lax.rsqrt(spread + EPSILON) * weights


def slot_r(k):
    return (OWN - k) % NZ


def slot_l(k):
    return (OWN + k) % NZ


def kernel(
    patches,
    visible,
    counts,
    pos_embed,
    mask_token,
    enc_gain,
    enc_qkv,
    enc_wo,
    enc_to_dec,
    dec_gain,
    dec_qkv,
    dec_wo,
    out,
    patch_v,
    pos_v,
    wo_v,
    e2d_v,
    dqkv_v,
    dwo_v,
    w_all,
    x_all,
    x_own,
    kv_all,
    q_all,
    o_first,
    m_first,
    l_first,
    mix_own,
    mix_send,
    mix_recv,
    dn_all,
    dec_in,
    dkv,
    dmix,
    load_sem,
    zs,
    zr,
    ws,
    wr,
    cs,
    cr,
    rs,
    rr,
    hs,
    hr,
):
    v = lax.axis_index("vol")
    z = lax.axis_index("seq")
    core = v % NC
    y = (v // NC) % NY
    x = v // (NC * NY)
    part = z % 2

    def vol_of(px, py, pc):
        return (px * NY + py) * NC + pc

    right = (v, (z + 1) % NZ)
    left = (v, (z + NZ - 1) % NZ)
    mate = (v, z + 1 - 2 * part)
    up = (vol_of(x, (y + 1) % NY, core), z)
    down = (vol_of(x, (y + NY - 1) % NY, core), z)
    sibling = (vol_of(x, y, 1 - core), z)
    x_dev = [(vol_of((x + i) % NX, y, core), z) for i in range(NX)]

    barrier = pltpu.get_barrier_semaphore()
    partners = [right, left, up, down, sibling] + x_dev[1:]
    for device in partners:
        pl.semaphore_signal(barrier, inc=1, device_id=device, device_id_type=MESH)

    loads = {}

    def load(name, src, dst, index):
        copy = pltpu.make_async_copy(src, dst, load_sem.at[index])
        copy.start()
        loads[name] = copy

    for i in range(3):
        column = pl.multiple_of(i * HA + part * HG, 128)
        load(
            "w%d" % i,
            enc_qkv.at[:, pl.ds(column, HG)],
            w_all.at[x, y, core, :, pl.ds(i * HG, HG)],
            i,
        )
    load("patches", patches, patch_v, 3)
    load("pos", pos_embed, pos_v, 4)
    load("wo", enc_wo, wo_v, 5)
    load("e2d", enc_to_dec, e2d_v, 6)
    load("dqkv", dec_qkv, dqkv_v, 7)
    load("dwo", dec_wo, dwo_v, 8)

    sends = []

    def remote(src, dst, send_sem, recv_sem, device):
        copy = pltpu.make_async_remote_copy(
            src_ref=src,
            dst_ref=dst,
            send_sem=send_sem,
            recv_sem=recv_sem,
            device_id=device,
            device_id_type=MESH,
        )
        return copy

    def start(copy):
        copy.start()
        sends.append(copy)

    def z_copy(k, h, to_right):
        rows = pl.ds(h * HALF, HALF)
        slot = slot_r if to_right else slot_l
        side = 0 if to_right else 1
        index = ((k - 1) * 2 + h) * 2 + side
        return remote(
            x_all.at[slot(k - 1), rows],
            x_all.at[slot(k), rows],
            zs.at[index],
            zr.at[index],
            right if to_right else left,
        )

    def z_has(k, h, to_right):
        return k < 6 or (k == 6 and (h == 0) == to_right)

    def z_event(k, h):
        for to_right in (True, False):
            if z_has(k, h, to_right):
                z_copy(k, h, to_right).wait_recv()
                if z_has(k + 1, h, to_right):
                    start(z_copy(k + 1, h, to_right))

    def wx_copy(i, other):
        cell = w_all.at[other, y, core]
        return remote(cell, cell, ws.at[i - 1], wr.at[i - 1], x_dev[i])

    def wy_copy(j, h, upward):
        owner = (y + NY - (j - 1)) % NY if upward else (y + j - 1) % NY
        cell = w_all.at[pl.ds(h * 2, 2), owner, core]
        index = NX - 1 + ((j - 1) * 2 + h) * 2 + (0 if upward else 1)
        return remote(cell, cell, ws.at[index], wr.at[index], up if upward else down)

    def wy_has(j, h, upward):
        return j < 4 or (j == 4 and (h == 0) == upward)

    def wy_recv(j, h, upward):
        owner = (y + NY - j) % NY if upward else (y + j) % NY
        cell = w_all.at[pl.ds(h * 2, 2), owner, core]
        index = NX - 1 + ((j - 1) * 2 + h) * 2 + (0 if upward else 1)
        remote(cell, cell, ws.at[index], wr.at[index], up if upward else down).wait_recv()

    def wc_copy(offset, of_core):
        cell = w_all.at[:, (y + offset) % NY, of_core]
        return remote(cell, cell, cs.at[offset], cr.at[offset], sibling)

    def wx_event():
        for i in range(1, NX):
            cell = w_all.at[(x + NX - i) % NX, y, core]
            remote(cell, cell, ws.at[i - 1], wr.at[i - 1], x_dev[i]).wait_recv()
        for h in range(2):
            for upward in (True, False):
                start(wy_copy(1, h, upward))
        start(wc_copy(0, core))

    def wy_event(j, h):
        for upward in (True, False):
            if wy_has(j, h, upward):
                wy_recv(j, h, upward)
                if wy_has(j + 1, h, upward):
                    start(wy_copy(j + 1, h, upward))
        if h == 1:
            start(wc_copy(j, core))
            if j < 4:
                start(wc_copy(NY - j, core))

    for i in range(3):
        loads["w%d" % i].wait()
    pl.semaphore_wait(barrier, len(partners))
    for i in range(1, NX):
        start(wx_copy(i, x))

    loads["patches"].wait()
    token = lax.broadcasted_iota(jnp.int32, (TOK, CAP), 0)
    slot = lax.broadcasted_iota(jnp.int32, (TOK, CAP), 1)
    chooser = visible[...] == token
    chosen = jnp.where(chooser, 1.0, 0.0)
    x_vis = dot(jnp.transpose(chosen).astype(BF), patch_v[...])
    x_own[...] = x_vis
    normed = layer_norm(x_vis, enc_gain[...].astype(F32)).astype(BF)
    x_all[OWN] = normed
    for h in range(2):
        for to_right in (True, False):
            start(z_copy(1, h, to_right))

    count = counts[0, z]
    live_chosen = jnp.where(chooser & (slot < count), 1.0, 0.0)
    is_visible = jnp.sum(live_chosen, axis=1, keepdims=True) > 0.5

    key_index = lax.broadcasted_iota(jnp.int32, (1, NZ * CAP), 1)
    limit = jnp.zeros((1, NZ * CAP), jnp.int32)
    for e in range(NZ):
        limit = jnp.where(
            key_index >= e * CAP, e * CAP + counts[0, (z + e + NZ - OWN) % NZ], limit
        )
    bias = jnp.where(key_index < limit, 0.0, NEGATIVE)

    wx_event()
    z_event(1, 0)
    wy_event(1, 0)
    wy_event(1, 1)
    z_event(1, 1)
    wy_event(2, 0)
    z_event(2, 0)
    wy_event(2, 1)
    wy_event(3, 0)
    z_event(2, 1)
    wy_event(3, 1)
    z_event(3, 0)
    wy_event(4, 0)
    wy_event(4, 1)
    for offset in range(NY):
        wc_copy(offset, 1 - core).wait_recv()
    z_event(3, 1)

    weights = w_all.reshape(D, WG)

    def project(first, last):
        rows = x_all[first:last].reshape((last - first) * CAP, D)
        kv_all[first * CAP : last * CAP, :] = dot(rows, weights[:, HG:]).astype(BF)

    lane = lax.broadcasted_iota(jnp.int32, (2 * CAP, 128), 1) // 64

    mate_slot = OWN + 1 - 2 * part
    pair = jnp.concatenate([x_all[mate_slot], x_all[OWN]], axis=0)
    q_all[...] = (dot(pair, weights[:, :HG]).astype(BF) * 0.125).astype(BF)
    project(1, 8)
    z_event(4, 0)
    z_event(4, 1)
    project(0, 1)
    project(8, 9)

    def attend(pair_index, first, last):
        cols = slice(pair_index * 128, (pair_index + 1) * 128)
        queries = q_all[:, cols]
        keys = kv_all[first * CAP : last * CAP, cols]
        values = kv_all[first * CAP : last * CAP, HG + pair_index * 128 : HG + (pair_index + 1) * 128]
        row_bias = bias[:, first * CAP : last * CAP]
        parts = []
        for s in range(2):
            one = jnp.where(lane == s, queries, jnp.zeros_like(queries))
            scores = dot_nt(one, keys) + row_bias
            top = jnp.max(scores, axis=-1, keepdims=True)
            raised = jnp.exp(scores - top)
            total = jnp.sum(raised, axis=-1, keepdims=True)
            parts.append((top, total, dot(raised.astype(BF), values)))
        (t0, l0, o0), (t1, l1, o1) = parts
        return (
            jnp.where(lane == 0, t0, t1),
            jnp.where(lane == 0, l0, l1),
            jnp.where(lane == 0, o0, o1),
        )

    def first_part(p):
        cols = slice(p * 128, (p + 1) * 128)
        top, total, mixed = attend(p, 0, FIRST)
        m_first[:, cols] = top
        l_first[:, cols] = total
        o_first[:, cols] = mixed

    first_part(0)
    z_event(5, 0)
    first_part(1)
    z_event(5, 1)
    first_part(2)
    z_event(6, 0)
    z_event(6, 1)
    project(FIRST, NZ)
    for p in range(3):
        cols = slice(p * 128, (p + 1) * 128)
        top, total, mixed = attend(p, FIRST, NZ)
        old = m_first[:, cols]
        new = jnp.maximum(old, top)
        a, b = jnp.exp(old - new), jnp.exp(top - new)
        mixed = o_first[:, cols] * a + mixed * b
        total = l_first[:, cols] * a + total * b
        mixed = (mixed / total).astype(BF)
        mix_send[:, cols] = mixed[:CAP]
        mix_own[:, cols] = mixed[CAP:]

    back = remote(mix_send, mix_recv, rs, rr, mate)
    start(back)
    loads["wo"].wait()
    own_rows = pl.multiple_of(part * HG, 128)
    mate_rows = pl.multiple_of((1 - part) * HG, 128)
    enc_out = x_own[...] + dot(mix_own[...], wo_v[pl.ds(own_rows, HG), :])
    loads["e2d"].wait()
    loads["pos"].wait()
    loads["dqkv"].wait()
    loads["dwo"].wait()
    back.wait_recv()
    enc_out = enc_out + dot(mix_recv[...], wo_v[pl.ds(mate_rows, HG), :])
    latent = dot(enc_out.astype(BF), e2d_v[...]).astype(BF)
    placed = dot(live_chosen.astype(BF), latent)
    dec = jnp.where(is_visible, placed, mask_token[...].astype(F32)) + pos_v[...].astype(F32)
    dec_in[...] = dec
    dnorm = layer_norm(dec, dec_gain[...].astype(F32)).astype(BF)
    dn_all[1] = dnorm[:LAYER]
    dn_all[2] = dnorm[LAYER:]
    halo_r = remote(dn_all.at[2], dn_all.at[0], hs.at[0], hr.at[0], right)
    halo_l = remote(dn_all.at[1], dn_all.at[3], hs.at[1], hr.at[1], left)
    start(halo_r)
    start(halo_l)

    proj = dot(dnorm, dqkv_v[...]).astype(BF)
    dq = proj[:, :DD]
    dkv[LAYER : LAYER + TOK, :] = proj[:, DD:]
    scale = LOG2E / math.sqrt(DD // DHEADS)
    quad_lane = lax.broadcasted_iota(jnp.int32, (TOK, 128), 1) // 32

    def quad(queries, keys, values, row_bias, lanes):
        top = total = mixed = None
        for s in range(4):
            one = jnp.where(lanes == s, queries, jnp.zeros_like(queries))
            scores = dot_nt(one, keys) * scale
            if row_bias is not None:
                scores = scores + row_bias
            t = jnp.max(scores, axis=-1, keepdims=True)
            raised = jnp.exp2(scores - t)
            l = jnp.sum(raised, axis=-1, keepdims=True)
            o = dot(raised.astype(BF), values)
            if s == 0:
                top = jnp.broadcast_to(t, o.shape)
                total = jnp.broadcast_to(l, o.shape)
                mixed = o
            else:
                top = jnp.where(lanes == s, t, top)
                total = jnp.where(lanes == s, l, total)
                mixed = jnp.where(lanes == s, o, mixed)
        return top, total, mixed

    local = []
    for g in range(4):
        cols = slice(g * 128, (g + 1) * 128)
        local.append(
            quad(
                dq[:, cols],
                dkv[LAYER : LAYER + TOK, cols],
                dkv[LAYER : LAYER + TOK, DD + g * 128 : DD + (g + 1) * 128],
                None,
                quad_lane,
            )
        )

    halo_r.wait_recv()
    halo_l.wait_recv()
    dkv[:LAYER, :] = dot(dn_all[0], dqkv_v[:, DD:]).astype(BF)
    dkv[LAYER + TOK :, :] = dot(dn_all[3], dqkv_v[:, DD:]).astype(BF)
    low_bias = jnp.where(z == 0, NEGATIVE, 0.0)
    high_bias = jnp.where(z == NZ - 1, NEGATIVE, 0.0)
    half_lane = quad_lane[:LAYER]
    for g in range(4):
        cols = slice(g * 128, (g + 1) * 128)
        value_cols = slice(DD + g * 128, DD + (g + 1) * 128)
        for level in range(2):
            rows = slice(level * LAYER, (level + 1) * LAYER)
            key_rows = slice(0, LAYER) if level == 0 else slice(LAYER + TOK, 2 * LAYER + TOK)
            top, total, mixed = quad(
                dq[rows, cols],
                dkv[key_rows, cols],
                dkv[key_rows, value_cols],
                low_bias if level == 0 else high_bias,
                half_lane,
            )
            old = local[g][0][rows]
            new = jnp.maximum(old, top)
            a, b = jnp.exp2(old - new), jnp.exp2(top - new)
            mixed = local[g][2][rows] * a + mixed * b
            total = local[g][1][rows] * a + total * b
            dmix[rows, cols] = (mixed / total).astype(BF)
    out[...] = (dec_in[...] + dot(dmix[...], dwo_v[...])).astype(BF)

    for copy in sends:
        copy.wait_send()


def local(
    patches,
    visible,
    counts,
    pos_embed,
    mask_token,
    enc_gain,
    enc_qkv,
    enc_wo,
    enc_to_dec,
    dec_gain,
    dec_qkv,
    dec_wo,
):
    vm = pl.BlockSpec(memory_space=pltpu.VMEM)
    sm = pl.BlockSpec(memory_space=pltpu.SMEM)
    hbm = pl.BlockSpec(memory_space=pl.ANY)
    dma = pltpu.SemaphoreType.DMA
    decoded = pl.pallas_call(
        kernel,
        out_shape=jax.ShapeDtypeStruct((TOK, DD), BF),
        in_specs=[hbm, vm, sm, hbm, vm, vm, hbm, hbm, hbm, vm, hbm, hbm],
        out_specs=vm,
        scratch_shapes=[
            pltpu.VMEM((TOK, D), BF),
            pltpu.VMEM((TOK, DD), BF),
            pltpu.VMEM((HA, D), BF),
            pltpu.VMEM((D, DD), BF),
            pltpu.VMEM((DD, 3 * DD), BF),
            pltpu.VMEM((DD, DD), BF),
            pltpu.VMEM((NX, NY, NC, ROWS, WG), BF),
            pltpu.VMEM((NZ, CAP, D), BF),
            pltpu.VMEM((CAP, D), F32),
            pltpu.VMEM((NZ * CAP, 2 * HG), BF),
            pltpu.VMEM((2 * CAP, HG), BF),
            pltpu.VMEM((2 * CAP, HG), F32),
            pltpu.VMEM((2 * CAP, HG), F32),
            pltpu.VMEM((2 * CAP, HG), F32),
            pltpu.VMEM((CAP, HG), BF),
            pltpu.VMEM((CAP, HG), BF),
            pltpu.VMEM((CAP, HG), BF),
            pltpu.VMEM((4, LAYER, DD), BF),
            pltpu.VMEM((TOK, DD), F32),
            pltpu.VMEM((2 * LAYER + TOK, 2 * DD), BF),
            pltpu.VMEM((TOK, DD), BF),
            dma((9,)),
            dma((24,)),
            dma((24,)),
            dma((NX - 1 + 16,)),
            dma((NX - 1 + 16,)),
            dma((NY,)),
            dma((NY,)),
            dma,
            dma,
            dma((2,)),
            dma((2,)),
        ],
        compiler_params=pltpu.CompilerParams(
            collective_id=0, has_side_effects=True, vmem_limit_bytes=48 * 2**20
        ),
        cost_estimate=pl.CostEstimate(
            flops=3 * 10**9, bytes_accessed=10 * 2**20, transcendentals=3 * 10**6
        ),
        name="volume",
    )(
        patches[0],
        visible[0],
        counts,
        pos_embed,
        mask_token[None],
        enc_gain[None],
        enc_qkv,
        enc_wo,
        enc_to_dec,
        dec_gain[None],
        dec_qkv,
        dec_wo,
    )
    return decoded[None]


def solution(mesh):
    in_specs = (
        P("vol", "seq", None),
        P("vol", "seq", None),
        P("vol", None),
        P("seq", None),
        P(),
        P(),
        P("vol", None),
        P(),
        P(),
        P(),
        P(),
        P(),
    )
    out_specs = P("vol", "seq", None)
    return jax.shard_map(local, mesh=mesh, in_specs=in_specs, out_specs=out_specs, check_vma=False)
```

```python
import functools
import math

import jax
import jax.numpy as jnp
from jax import lax
from jax.experimental import pallas as pl
from jax.experimental.pallas import tpu as pltpu
from jax.sharding import PartitionSpec as P

MESH = pl.DeviceIdType.MESH
BF = jnp.bfloat16
F32 = jnp.float32

HEADS = 12
DHEADS = 16
NX, NY, NC, NZ = 4, 8, 2, 12
CAP = 96
TOK = 256
LAYER = 128
D = 1024
HA = 768
HG = HA // 2
WG = 3 * HG
DD = 512
ROWS = 16
HALF = CAP // 2
EPSILON = 1e-06
NEGATIVE = -1e30
OWN = 4
FIRST = 9
LOG2E = math.log2(math.e)


def dot(a, b):
    return jnp.dot(a, b, preferred_element_type=F32)


def dot_nt(a, b):
    return lax.dot_general(a, b, (((1,), (1,)), ((), ())), preferred_element_type=F32)


def layer_norm(values, weights):
    centred = values - jnp.mean(values, axis=-1, keepdims=True)
    spread = jnp.mean(centred * centred, axis=-1, keepdims=True)
    return centred * lax.rsqrt(spread + EPSILON) * weights


def slot_r(k):
    return (OWN - k) % NZ


def slot_l(k):
    return (OWN + k) % NZ


def kernel(
    patches,
    visible,
    counts,
    pos_embed,
    mask_token,
    enc_gain,
    enc_qkv,
    enc_wo,
    enc_to_dec,
    dec_gain,
    dec_qkv,
    dec_wo,
    out,
    patch_v,
    pos_v,
    wo_v,
    e2d_v,
    dqkv_v,
    dwo_v,
    w_all,
    x_all,
    x_own,
    k_all,
    q_all,
    bias,
    ewv_t,
    dwv_t,
    mix_own,
    mix_send,
    mix_recv,
    dn_all,
    dec_in,
    dq,
    dk,
    dv_t,
    dmix,
    load_sem,
    zs,
    zr,
    ws,
    wr,
    cs,
    cr,
    rs,
    rr,
    hs,
    hr,
):
    v = lax.axis_index("vol")
    z = lax.axis_index("seq")
    core = v % NC
    y = (v // NC) % NY
    x = v // (NC * NY)
    part = z % 2

    def vol_of(px, py, pc):
        return (px * NY + py) * NC + pc

    right = (v, (z + 1) % NZ)
    left = (v, (z + NZ - 1) % NZ)
    mate = (v, z + 1 - 2 * part)
    up = (vol_of(x, (y + 1) % NY, core), z)
    down = (vol_of(x, (y + NY - 1) % NY, core), z)
    sibling = (vol_of(x, y, 1 - core), z)
    x_dev = [(vol_of((x + i) % NX, y, core), z) for i in range(NX)]

    barrier = pltpu.get_barrier_semaphore()
    partners = [right, left, up, down, sibling] + x_dev[1:]
    for device in partners:
        pl.semaphore_signal(barrier, inc=1, device_id=device, device_id_type=MESH)

    loads = {}

    def load(name, src, dst, index):
        copy = pltpu.make_async_copy(src, dst, load_sem.at[index])
        copy.start()
        loads[name] = copy

    for i in range(3):
        column = pl.multiple_of(i * HA + part * HG, 128)
        load(
            "w%d" % i,
            enc_qkv.at[:, pl.ds(column, HG)],
            w_all.at[x, y, core, :, pl.ds(i * HG, HG)],
            i,
        )
    load("patches", patches, patch_v, 3)
    load("pos", pos_embed, pos_v, 4)
    load("wo", enc_wo, wo_v, 5)
    load("e2d", enc_to_dec, e2d_v, 6)
    load("dqkv", dec_qkv, dqkv_v, 7)
    load("dwo", dec_wo, dwo_v, 8)

    sends = []

    def remote(src, dst, send_sem, recv_sem, device):
        copy = pltpu.make_async_remote_copy(
            src_ref=src,
            dst_ref=dst,
            send_sem=send_sem,
            recv_sem=recv_sem,
            device_id=device,
            device_id_type=MESH,
        )
        return copy

    def start(copy):
        copy.start()
        sends.append(copy)

    def z_copy(k, h, to_right):
        rows = pl.ds(h * HALF, HALF)
        slot = slot_r if to_right else slot_l
        side = 0 if to_right else 1
        index = ((k - 1) * 2 + h) * 2 + side
        return remote(
            x_all.at[slot(k - 1), rows],
            x_all.at[slot(k), rows],
            zs.at[index],
            zr.at[index],
            right if to_right else left,
        )

    def z_has(k, h, to_right):
        return k < 6 or (k == 6 and (h == 0) == to_right)

    def z_event(k, h):
        for to_right in (True, False):
            if z_has(k, h, to_right):
                z_copy(k, h, to_right).wait_recv()
                if z_has(k + 1, h, to_right):
                    start(z_copy(k + 1, h, to_right))

    def wx_copy(i, other):
        cell = w_all.at[other, y, core]
        return remote(cell, cell, ws.at[i - 1], wr.at[i - 1], x_dev[i])

    def wy_copy(j, h, upward):
        owner = (y + NY - (j - 1)) % NY if upward else (y + j - 1) % NY
        cell = w_all.at[pl.ds(h * 2, 2), owner, core]
        index = NX - 1 + ((j - 1) * 2 + h) * 2 + (0 if upward else 1)
        return remote(cell, cell, ws.at[index], wr.at[index], up if upward else down)

    def wy_has(j, h, upward):
        return j < 4 or (j == 4 and (h == 0) == upward)

    def wy_recv(j, h, upward):
        owner = (y + NY - j) % NY if upward else (y + j) % NY
        cell = w_all.at[pl.ds(h * 2, 2), owner, core]
        index = NX - 1 + ((j - 1) * 2 + h) * 2 + (0 if upward else 1)
        remote(cell, cell, ws.at[index], wr.at[index], up if upward else down).wait_recv()

    def wc_copy(offset, h, of_core):
        cell = w_all.at[pl.ds(h * 2, 2), (y + offset) % NY, of_core]
        index = offset * 2 + h
        return remote(cell, cell, cs.at[index], cr.at[index], sibling)

    def wx_event():
        for i in range(1, NX):
            cell = w_all.at[(x + NX - i) % NX, y, core]
            remote(cell, cell, ws.at[i - 1], wr.at[i - 1], x_dev[i]).wait_recv()
        for h in range(2):
            for upward in (True, False):
                start(wy_copy(1, h, upward))
        for h in range(2):
            start(wc_copy(0, h, core))

    def wy_event(j, h):
        for upward in (True, False):
            if wy_has(j, h, upward):
                wy_recv(j, h, upward)
                if wy_has(j + 1, h, upward):
                    start(wy_copy(j + 1, h, upward))
                start(wc_copy(NY - j if upward else j, h, core))

    for i in range(3):
        loads["w%d" % i].wait()
    pl.semaphore_wait(barrier, len(partners))
    for i in range(1, NX):
        start(wx_copy(i, x))

    loads["patches"].wait()
    token = lax.broadcasted_iota(jnp.int32, (TOK, CAP), 0)
    slot = lax.broadcasted_iota(jnp.int32, (TOK, CAP), 1)
    chooser = visible[...] == token
    chosen = jnp.where(chooser, 1.0, 0.0)
    x_vis = dot(jnp.transpose(chosen).astype(BF), patch_v[...])
    x_own[...] = x_vis
    normed = layer_norm(x_vis, enc_gain[...].astype(F32)[None]).astype(BF)
    x_all[OWN] = normed
    for h in range(2):
        for to_right in (True, False):
            start(z_copy(1, h, to_right))

    count = counts[0, z]
    live_chosen = jnp.where(chooser & (slot < count), 1.0, 0.0)
    is_visible = jnp.sum(live_chosen, axis=1, keepdims=True) > 0.5

    slot_row = lax.broadcasted_iota(jnp.int32, (CAP, 128), 0)
    for e in range(NZ):
        alive = slot_row < counts[0, (z + e + NZ - OWN) % NZ]
        bias[e * CAP : (e + 1) * CAP, :] = jnp.where(alive, 0.0, NEGATIVE)
    loads["dqkv"].wait()
    dwv_t[...] = jnp.transpose(dqkv_v[:, 2 * DD :])

    wx_event()
    z_event(1, 0)
    wy_event(1, 0)
    z_event(1, 1)
    wy_event(1, 1)
    z_event(2, 0)
    wy_event(2, 0)
    z_event(2, 1)
    wy_event(2, 1)
    z_event(3, 0)
    wy_event(3, 0)
    z_event(3, 1)
    wy_event(3, 1)
    wy_event(4, 0)
    wy_event(4, 1)
    z_event(4, 0)
    for offset in range(NY):
        for h in range(2):
            wc_copy(offset, h, 1 - core).wait_recv()

    weights = w_all.reshape(D, WG)

    def project_keys(first, last):
        rows = x_all[first:last].reshape((last - first) * CAP, D)
        keys = dot(rows, weights[:, HG : 2 * HG]).astype(BF)
        k_all[first * CAP : last * CAP, :] = keys

    def project_values(first, last):
        rows = x_all[first:last].reshape((last - first) * CAP, D)
        return dot_nt(ewv_t[...], rows).astype(BF)

    lane = lax.broadcasted_iota(jnp.int32, (2 * CAP, 128), 1) // 64

    mate_slot = OWN + 1 - 2 * part
    pair = jnp.concatenate([x_all[mate_slot], x_all[OWN]], axis=0)
    queries = (dot(pair, weights[:, :HG]).astype(BF) * 0.125).astype(BF)
    for p in range(3):
        two = queries[:, p * 128 : (p + 1) * 128]
        for s in range(2):
            one = jnp.where(lane == s, two, jnp.zeros_like(two))
            q_all[p, s * 2 * CAP : (s + 1) * 2 * CAP, :] = one
    ewv_t[...] = jnp.transpose(weights[:, 2 * HG :])
    project_keys(1, 8)
    z_event(4, 1)
    project_keys(0, 1)
    project_keys(8, 9)

    def attend(p, first, last, values_t):
        cols = slice(p * 128, (p + 1) * 128)
        row_bias = bias[first * CAP : last * CAP, :]
        scores = dot_nt(k_all[first * CAP : last * CAP, cols], q_all[p])
        scores = scores + jnp.concatenate([row_bias] * 3, axis=1)
        top = jnp.max(scores, axis=0, keepdims=True)
        raised = jnp.exp(scores - top)
        total = jnp.sum(raised, axis=0, keepdims=True)
        return top, total, dot(values_t[cols, :], raised.astype(BF))

    state = {}

    def first_part(p):
        state[p] = attend(p, 0, FIRST, values_first)

    def next_part(p, first, last, values_t):
        old, old_total, old_mixed = state[p]
        top, total, mixed = attend(p, first, last, values_t)
        new = jnp.maximum(old, top)
        a, b = jnp.exp(old - new), jnp.exp(top - new)
        state[p] = (new, old_total * a + total * b, old_mixed * a + mixed * b)

    values_first = project_values(0, FIRST)
    first_part(0)
    z_event(5, 0)
    first_part(1)
    z_event(5, 1)
    first_part(2)
    z_event(6, 0)
    z_event(6, 1)
    project_keys(FIRST, NZ)
    values_last = project_values(FIRST, NZ)
    for p in range(3):
        next_part(p, FIRST, NZ, values_last)
        _, total, mixed = state[p]
        turned = jnp.transpose(mixed / total)
        joined = jnp.where(lane == 0, turned[: 2 * CAP], turned[2 * CAP :]).astype(BF)
        cols = slice(p * 128, (p + 1) * 128)
        mix_send[:, cols] = joined[:CAP]
        mix_own[:, cols] = joined[CAP:]

    back = remote(mix_send, mix_recv, rs, rr, mate)
    start(back)
    loads["wo"].wait()
    own_rows = pl.multiple_of(part * HG, 128)
    mate_rows = pl.multiple_of((1 - part) * HG, 128)
    enc_out = x_own[...] + dot(mix_own[...], wo_v[pl.ds(own_rows, HG), :])
    loads["e2d"].wait()
    loads["pos"].wait()
    loads["dwo"].wait()
    back.wait_recv()
    enc_out = enc_out + dot(mix_recv[...], wo_v[pl.ds(mate_rows, HG), :])
    latent = dot(enc_out.astype(BF), e2d_v[...]).astype(BF)
    placed = dot(live_chosen.astype(BF), latent)
    dec = jnp.where(is_visible, placed, mask_token[...].astype(F32)[None]) + pos_v[...].astype(F32)
    dec_in[...] = dec
    dnorm = layer_norm(dec, dec_gain[...].astype(F32)[None]).astype(BF)
    dn_all[1] = dnorm[:LAYER]
    dn_all[2] = dnorm[LAYER:]
    halo_r = remote(dn_all.at[2], dn_all.at[0], hs.at[0], hr.at[0], right)
    halo_l = remote(dn_all.at[1], dn_all.at[3], hs.at[1], hr.at[1], left)
    start(halo_r)
    start(halo_l)

    proj = dot(dnorm, dqkv_v[:, : 2 * DD]).astype(BF)
    dk[LAYER : LAYER + TOK, :] = proj[:, DD:]
    dv_t[:, LAYER : LAYER + TOK] = dot_nt(dwv_t[...], dnorm).astype(BF)
    scale = LOG2E / math.sqrt(DD // DHEADS)
    quad_lane = lax.broadcasted_iota(jnp.int32, (TOK, 128), 1) // 32
    for g in range(4):
        four = proj[:, g * 128 : (g + 1) * 128]
        for s in range(4):
            one = jnp.where(quad_lane == s, four, jnp.zeros_like(four))
            for level in range(2):
                dq[g, level, s * LAYER : (s + 1) * LAYER, :] = one[level * LAYER : (level + 1) * LAYER]

    def quad(g, level, first, last, off_grid):
        scores = dot_nt(dk[first:last, g * 128 : (g + 1) * 128], dq[g, level]) * scale
        if off_grid is not None:
            scores = scores + off_grid
        top = jnp.max(scores, axis=0, keepdims=True)
        raised = jnp.exp2(scores - top)
        total = jnp.sum(raised, axis=0, keepdims=True)
        weight = raised.astype(BF)
        mixed = []
        for s in range(4):
            head = (g * 4 + s) * 32
            mixed.append(dot(dv_t[head : head + 32, first:last], weight[:, s * LAYER : (s + 1) * LAYER]))
        return top, total, mixed

    inner = {}
    for g in range(4):
        for level in range(2):
            inner[g, level] = quad(g, level, LAYER, LAYER + TOK, None)

    edges = ((0, LAYER), (LAYER + TOK, 2 * LAYER + TOK))
    halo_r.wait_recv()
    halo_l.wait_recv()
    for level, (first, last) in enumerate(edges):
        rows = dn_all[3 * level]
        dk[first:last, :] = dot(rows, dqkv_v[:, DD : 2 * DD]).astype(BF)
        dv_t[:, first:last] = dot_nt(dwv_t[...], rows).astype(BF)
    off = (jnp.where(z == 0, NEGATIVE, 0.0), jnp.where(z == NZ - 1, NEGATIVE, 0.0))
    for g in range(4):
        for level, (first, last) in enumerate(edges):
            old, old_total, old_mixed = inner[g, level]
            top, total, mixed = quad(g, level, first, last, off[level])
            new = jnp.maximum(old, top)
            a, b = jnp.exp2(old - new), jnp.exp2(top - new)
            share = 1.0 / (old_total * a + total * b)
            a, b = a * share, b * share
            heads = []
            for s in range(4):
                at = slice(s * LAYER, (s + 1) * LAYER)
                heads.append(old_mixed[s] * a[:, at] + mixed[s] * b[:, at])
            turned = jnp.transpose(jnp.concatenate(heads, axis=0))
            dmix[level * LAYER : (level + 1) * LAYER, g * 128 : (g + 1) * 128] = turned.astype(BF)
    out[...] = (dec_in[...] + dot(dmix[...], dwo_v[...])).astype(BF)

    for copy in sends:
        copy.wait_send()


def local(
    patches,
    visible,
    counts,
    pos_embed,
    mask_token,
    enc_gain,
    enc_qkv,
    enc_wo,
    enc_to_dec,
    dec_gain,
    dec_qkv,
    dec_wo,
):
    vm = pl.BlockSpec(memory_space=pltpu.VMEM)
    sm = pl.BlockSpec(memory_space=pltpu.SMEM)
    hbm = pl.BlockSpec(memory_space=pl.ANY)
    dma = pltpu.SemaphoreType.DMA
    decoded = pl.pallas_call(
        kernel,
        out_shape=jax.ShapeDtypeStruct((TOK, DD), BF),
        in_specs=[hbm, vm, sm, hbm, vm, vm, hbm, hbm, hbm, vm, hbm, hbm],
        out_specs=vm,
        scratch_shapes=[
            pltpu.VMEM((TOK, D), BF),
            pltpu.VMEM((TOK, DD), BF),
            pltpu.VMEM((HA, D), BF),
            pltpu.VMEM((D, DD), BF),
            pltpu.VMEM((DD, 3 * DD), BF),
            pltpu.VMEM((DD, DD), BF),
            pltpu.VMEM((NX, NY, NC, ROWS, WG), BF),
            pltpu.VMEM((NZ, CAP, D), BF),
            pltpu.VMEM((CAP, D), F32),
            pltpu.VMEM((NZ * CAP, HG), BF),
            pltpu.VMEM((3, 4 * CAP, 128), BF),
            pltpu.VMEM((NZ * CAP, 128), F32),
            pltpu.VMEM((HG, D), BF),
            pltpu.VMEM((DD, DD), BF),
            pltpu.VMEM((CAP, HG), BF),
            pltpu.VMEM((CAP, HG), BF),
            pltpu.VMEM((CAP, HG), BF),
            pltpu.VMEM((4, LAYER, DD), BF),
            pltpu.VMEM((TOK, DD), F32),
            pltpu.VMEM((4, 2, 4 * LAYER, 128), BF),
            pltpu.VMEM((2 * LAYER + TOK, DD), BF),
            pltpu.VMEM((DD, 2 * LAYER + TOK), BF),
            pltpu.VMEM((TOK, DD), BF),
            dma((9,)),
            dma((24,)),
            dma((24,)),
            dma((NX - 1 + 16,)),
            dma((NX - 1 + 16,)),
            dma((2 * NY,)),
            dma((2 * NY,)),
            dma,
            dma,
            dma((2,)),
            dma((2,)),
        ],
        compiler_params=pltpu.CompilerParams(
            collective_id=0, has_side_effects=True, vmem_limit_bytes=60 * 2**20
        ),
        cost_estimate=pl.CostEstimate(
            flops=3 * 10**9, bytes_accessed=10 * 2**20, transcendentals=3 * 10**6
        ),
        name="volume",
    )(
        patches[0],
        visible[0],
        counts,
        pos_embed,
        mask_token,
        enc_gain,
        enc_qkv,
        enc_wo,
        enc_to_dec,
        dec_gain,
        dec_qkv,
        dec_wo,
    )
    return decoded[None]


def solution(mesh):
    in_specs = (
        P("vol", "seq", None),
        P("vol", "seq", None),
        P("vol", None),
        P("seq", None),
        P(),
        P(),
        P("vol", None),
        P(),
        P(),
        P(),
        P(),
        P(),
    )
    out_specs = P("vol", "seq", None)
    return jax.shard_map(local, mesh=mesh, in_specs=in_specs, out_specs=out_specs, check_vma=False)
```

```python
import functools
import math

import jax
import jax.numpy as jnp
from jax import lax
from jax.experimental import pallas as pl
from jax.experimental.pallas import tpu as pltpu
from jax.sharding import PartitionSpec as P

MESH = pl.DeviceIdType.MESH
BF = jnp.bfloat16
F32 = jnp.float32

HEADS = 12
DHEADS = 16
NX, NY, NC, NZ = 4, 8, 2, 12
CAP = 96
TOK = 256
LAYER = 128
D = 1024
HA = 768
HD = HA // HEADS
HG = HA // 2
WG = 3 * HG
DD = 512
ROWS = 16
HALF = CAP // 2
EPSILON = 1e-06
NEGATIVE = -1e30
OFFSETS = (-3, -2, -1, 0, 1, 2, 3, -4, 4, -5, 5, 6)
OWN = 3
FIRST = 7
SECOND = 11
LOG2E = math.log2(math.e)


def dot(a, b):
    return jnp.dot(a, b, preferred_element_type=F32)


def dot_nt(a, b):
    return lax.dot_general(a, b, (((1,), (1,)), ((), ())), preferred_element_type=F32)


def layer_norm(values, weights):
    centred = values - jnp.mean(values, axis=-1, keepdims=True)
    spread = jnp.mean(centred * centred, axis=-1, keepdims=True)
    return centred * lax.rsqrt(spread + EPSILON) * weights


def slot_r(k):
    return OFFSETS.index(-k) if k < 6 else NZ - 1


def slot_l(k):
    return OFFSETS.index(k)


def kernel(
    patches,
    visible,
    counts,
    pos_embed,
    mask_token,
    enc_gain,
    enc_qkv,
    enc_wo,
    enc_to_dec,
    dec_gain,
    dec_qkv,
    dec_wo,
    out,
    patch_v,
    pos_v,
    wo_v,
    e2d_v,
    dqkv_v,
    dwo_v,
    w_all,
    x_all,
    x_own,
    k_all,
    q_all,
    bias,
    ewv_t,
    dwv_t,
    mix_own,
    mix_send,
    mix_recv,
    dn_all,
    dec_in,
    dq,
    dk,
    dv_t,
    dmix,
    load_sem,
    zs,
    zr,
    ws,
    wr,
    cs,
    cr,
    rs,
    rr,
    hs,
    hr,
):
    v = lax.axis_index("vol")
    z = lax.axis_index("seq")
    core = v % NC
    y = (v // NC) % NY
    x = v // (NC * NY)
    part = z % 2

    def vol_of(px, py, pc):
        return (px * NY + py) * NC + pc

    right = (v, (z + 1) % NZ)
    left = (v, (z + NZ - 1) % NZ)
    mate = (v, z + 1 - 2 * part)
    up = (vol_of(x, (y + 1) % NY, core), z)
    down = (vol_of(x, (y + NY - 1) % NY, core), z)
    sibling = (vol_of(x, y, 1 - core), z)
    x_dev = [(vol_of((x + i) % NX, y, core), z) for i in range(NX)]

    barrier = pltpu.get_barrier_semaphore()
    partners = [right, left, up, down, sibling] + x_dev[1:]
    for device in partners:
        pl.semaphore_signal(barrier, inc=1, device_id=device, device_id_type=MESH)

    loads = {}

    def load(name, src, dst, index):
        copy = pltpu.make_async_copy(src, dst, load_sem.at[index])
        copy.start()
        loads[name] = copy

    for i in range(3):
        column = pl.multiple_of(i * HA + part * HG, 128)
        load(
            "w%d" % i,
            enc_qkv.at[:, pl.ds(column, HG)],
            w_all.at[x, y, core, :, pl.ds(i * HG, HG)],
            i,
        )
    load("patches", patches, patch_v, 3)
    load("pos", pos_embed, pos_v, 4)
    load("wo", enc_wo, wo_v, 5)
    load("e2d", enc_to_dec, e2d_v, 6)
    load("dqkv", dec_qkv, dqkv_v, 7)
    load("dwo", dec_wo, dwo_v, 8)

    sends = []

    def remote(src, dst, send_sem, recv_sem, device):
        copy = pltpu.make_async_remote_copy(
            src_ref=src,
            dst_ref=dst,
            send_sem=send_sem,
            recv_sem=recv_sem,
            device_id=device,
            device_id_type=MESH,
        )
        return copy

    def start(copy):
        copy.start()
        sends.append(copy)

    def z_copy(k, h, to_right):
        rows = pl.ds(h * HALF, HALF)
        slot = slot_r if to_right else slot_l
        side = 0 if to_right else 1
        index = ((k - 1) * 2 + h) * 2 + side
        return remote(
            x_all.at[slot(k - 1), rows],
            x_all.at[slot(k), rows],
            zs.at[index],
            zr.at[index],
            right if to_right else left,
        )

    def z_has(k, h, to_right):
        return k < 6 or (k == 6 and (h == 0) == to_right)

    def z_event(k, h):
        for to_right in (True, False):
            if z_has(k, h, to_right):
                z_copy(k, h, to_right).wait_recv()
                if z_has(k + 1, h, to_right):
                    start(z_copy(k + 1, h, to_right))


    def wx_copy(i, other):
        cell = w_all.at[other, y, core]
        return remote(cell, cell, ws.at[i - 1], wr.at[i - 1], x_dev[i])

    def wy_copy(j, h, upward, step):
        owner = (y + NY - step) % NY if upward else (y + step) % NY
        cell = w_all.at[pl.ds(h * 2, 2), owner, core]
        index = 3 + ((j - 1) * 2 + h) * 2 + (0 if upward else 1)
        return remote(cell, cell, ws.at[index], wr.at[index], up if upward else down)

    def wy_has(j, h, upward):
        return j < 4 or (j == 4 and (h == 0) == upward)

    def wc_copy(offset, h, of_core):
        cell = w_all.at[pl.ds(h * 2, 2), (y + offset) % NY, of_core]
        index = offset * 2 + h
        return remote(cell, cell, cs.at[index], cr.at[index], sibling)

    def wx_event():
        for i in range(1, NX):
            wx_copy(i, (x + NX - i) % NX).wait_recv()
        for h in range(2):
            for upward in (True, False):
                start(wy_copy(1, h, upward, 0))
        for h in range(2):
            start(wc_copy(0, h, core))

    def wy_event(j, h):
        for upward in (True, False):
            if wy_has(j, h, upward):
                wy_copy(j, h, upward, j).wait_recv()
                if wy_has(j + 1, h, upward):
                    start(wy_copy(j + 1, h, upward, j))
                start(wc_copy(NY - j if upward else j, h, core))

    def sibling_event():
        for offset in range(NY):
            for h in range(2):
                wc_copy(offset, h, 1 - core).wait_recv()

    for i in range(3):
        loads["w%d" % i].wait()
    pl.semaphore_wait(barrier, len(partners))
    for i in range(1, NX):
        start(wx_copy(i, x))

    loads["patches"].wait()
    token = lax.broadcasted_iota(jnp.int32, (TOK, CAP), 0)
    slot = lax.broadcasted_iota(jnp.int32, (TOK, CAP), 1)
    chooser = visible[...] == token
    chosen = jnp.where(chooser, 1.0, 0.0)
    x_vis = dot(jnp.transpose(chosen).astype(BF), patch_v[...])
    x_own[...] = x_vis
    normed = layer_norm(x_vis, enc_gain[...].astype(F32)[None]).astype(BF)
    x_all[OWN] = normed
    for h in range(2):
        for to_right in (True, False):
            start(z_copy(1, h, to_right))

    count = counts[0, z]
    live_chosen = jnp.where(chooser & (slot < count), 1.0, 0.0)
    is_visible = jnp.sum(live_chosen, axis=1, keepdims=True) > 0.5

    slot_row = lax.broadcasted_iota(jnp.int32, (CAP, 128), 0)
    for e in range(NZ):
        alive = slot_row < counts[0, (z + OFFSETS[e] + NZ) % NZ]
        bias[e * CAP : (e + 1) * CAP, :] = jnp.where(alive, 0.0, NEGATIVE)
    loads["dqkv"].wait()
    dwv_t[...] = jnp.transpose(dqkv_v[:, 2 * DD :])

    wx_event()
    z_event(1, 0)
    wy_event(1, 0)
    z_event(1, 1)
    wy_event(1, 1)
    z_event(2, 0)
    wy_event(2, 0)
    z_event(2, 1)
    wy_event(2, 1)
    z_event(3, 0)
    wy_event(3, 0)
    z_event(3, 1)
    wy_event(3, 1)
    z_event(4, 0)
    wy_event(4, 0)
    wy_event(4, 1)
    z_event(4, 1)
    sibling_event()
    z_event(5, 0)

    weights = w_all.reshape(D, WG)

    def project_keys(first, last):
        rows = x_all[first:last].reshape((last - first) * CAP, D)
        keys = dot(rows, weights[:, HG : 2 * HG]).astype(BF)
        k_all[first * CAP : last * CAP, :] = keys

    def project_values(first, last):
        rows = x_all[first:last].reshape((last - first) * CAP, D)
        return dot_nt(ewv_t[...], rows).astype(BF)

    lane = lax.broadcasted_iota(jnp.int32, (2 * CAP, 128), 1) // 64

    mate_slot = OWN + 1 - 2 * part
    pair = jnp.concatenate([x_all[mate_slot], x_all[OWN]], axis=0)
    queries = (dot(pair, weights[:, :HG]) * (LOG2E / math.sqrt(HD))).astype(BF)
    for p in range(3):
        two = queries[:, p * 128 : (p + 1) * 128]
        for s in range(2):
            one = jnp.where(lane == s, two, jnp.zeros_like(two))
            q_all[p, s * 2 * CAP : (s + 1) * 2 * CAP, :] = one
    ewv_t[...] = jnp.transpose(weights[:, 2 * HG :])
    project_keys(0, FIRST)

    def attend(p, first, last, values_t):
        cols = slice(p * 128, (p + 1) * 128)
        row_bias = bias[first * CAP : last * CAP, :]
        scores = dot_nt(k_all[first * CAP : last * CAP, cols], q_all[p])
        scores = scores + jnp.concatenate([row_bias] * 3, axis=1)
        top = jnp.max(scores, axis=0, keepdims=True)
        raised = jnp.exp2(scores - top)
        total = jnp.sum(raised, axis=0, keepdims=True)
        return top, total, dot(values_t[cols, :], raised.astype(BF))

    state = {}

    def first_part(p):
        state[p] = attend(p, 0, FIRST, values_first)

    def next_part(p, first, last, values_t):
        old, old_total, old_mixed = state[p]
        top, total, mixed = attend(p, first, last, values_t)
        new = jnp.maximum(old, top)
        a, b = jnp.exp2(old - new), jnp.exp2(top - new)
        state[p] = (new, old_total * a + total * b, old_mixed * a + mixed * b)

    z_event(5, 1)
    values_first = project_values(0, FIRST)
    for p in range(3):
        first_part(p)
    project_keys(FIRST, SECOND)
    values_second = project_values(FIRST, SECOND)
    for p in range(3):
        next_part(p, FIRST, SECOND, values_second)
    z_event(6, 0)
    z_event(6, 1)
    project_keys(SECOND, NZ)
    values_last = project_values(SECOND, NZ)
    for p in range(3):
        next_part(p, SECOND, NZ, values_last)
        _, total, mixed = state[p]
        turned = jnp.transpose(mixed / total)
        joined = jnp.where(lane == 0, turned[: 2 * CAP], turned[2 * CAP :]).astype(BF)
        cols = slice(p * 128, (p + 1) * 128)
        mix_send[:, cols] = joined[:CAP]
        mix_own[:, cols] = joined[CAP:]

    back = remote(mix_send, mix_recv, rs, rr, mate)
    early = list(sends)
    start(back)
    loads["wo"].wait()
    own_rows = pl.multiple_of(part * HG, 128)
    mate_rows = pl.multiple_of((1 - part) * HG, 128)
    enc_out = x_own[...] + dot(mix_own[...], wo_v[pl.ds(own_rows, HG), :])
    loads["e2d"].wait()
    loads["pos"].wait()
    loads["dwo"].wait()
    for copy in early:
        copy.wait_send()
    back.wait_recv()
    enc_out = enc_out + dot(mix_recv[...], wo_v[pl.ds(mate_rows, HG), :])
    latent = dot(enc_out.astype(BF), e2d_v[...]).astype(BF)
    placed = dot(live_chosen.astype(BF), latent)
    dec = jnp.where(is_visible, placed, mask_token[...].astype(F32)[None]) + pos_v[...].astype(F32)
    dec_in[...] = dec
    dnorm = layer_norm(dec, dec_gain[...].astype(F32)[None]).astype(BF)
    dn_all[1] = dnorm[:LAYER]
    dn_all[2] = dnorm[LAYER:]
    halo_r = remote(dn_all.at[2], dn_all.at[0], hs.at[0], hr.at[0], right)
    halo_l = remote(dn_all.at[1], dn_all.at[3], hs.at[1], hr.at[1], left)
    start(halo_r)
    start(halo_l)

    scale = LOG2E / math.sqrt(DD // DHEADS)
    proj = (dot(dnorm, dqkv_v[:, :DD]) * scale).astype(BF)
    dk[LAYER : LAYER + TOK, :] = dot(dnorm, dqkv_v[:, DD : 2 * DD]).astype(BF)
    dv_t[:, LAYER : LAYER + TOK] = dot_nt(dwv_t[...], dnorm).astype(BF)
    quad_lane = lax.broadcasted_iota(jnp.int32, (TOK, 128), 1) // 32
    for g in range(4):
        four = proj[:, g * 128 : (g + 1) * 128]
        for s in range(4):
            one = jnp.where(quad_lane == s, four, jnp.zeros_like(four))
            for level in range(2):
                dq[g, level, s * LAYER : (s + 1) * LAYER, :] = one[level * LAYER : (level + 1) * LAYER]

    def quad(g, level, first, last, off_grid):
        scores = dot_nt(dk[first:last, g * 128 : (g + 1) * 128], dq[g, level])
        if off_grid is not None:
            scores = scores + off_grid
        top = jnp.max(scores, axis=0, keepdims=True)
        raised = jnp.exp2(scores - top)
        total = jnp.sum(raised, axis=0, keepdims=True)
        weight = raised.astype(BF)
        wide = dot(dv_t[g * 128 : (g + 1) * 128, first:last], weight)
        mixed = [wide[s * 32 : (s + 1) * 32, s * LAYER : (s + 1) * LAYER] for s in range(4)]
        return top, total, mixed

    inner = {}
    for g in range(4):
        for level in range(2):
            inner[g, level] = quad(g, level, LAYER, LAYER + TOK, None)

    edges = ((0, LAYER), (LAYER + TOK, 2 * LAYER + TOK))
    halo_r.wait_recv()
    halo_l.wait_recv()
    for level, (first, last) in enumerate(edges):
        rows = dn_all[3 * level]
        dk[first:last, :] = dot(rows, dqkv_v[:, DD : 2 * DD]).astype(BF)
        dv_t[:, first:last] = dot_nt(dwv_t[...], rows).astype(BF)
    off = (jnp.where(z == 0, NEGATIVE, 0.0), jnp.where(z == NZ - 1, NEGATIVE, 0.0))
    for g in range(4):
        for level, (first, last) in enumerate(edges):
            old, old_total, old_mixed = inner[g, level]
            top, total, mixed = quad(g, level, first, last, off[level])
            new = jnp.maximum(old, top)
            a, b = jnp.exp2(old - new), jnp.exp2(top - new)
            share = 1.0 / (old_total * a + total * b)
            a, b = a * share, b * share
            heads = []
            for s in range(4):
                at = slice(s * LAYER, (s + 1) * LAYER)
                heads.append(old_mixed[s] * a[:, at] + mixed[s] * b[:, at])
            turned = jnp.transpose(jnp.concatenate(heads, axis=0))
            dmix[level * LAYER : (level + 1) * LAYER, g * 128 : (g + 1) * 128] = turned.astype(BF)
    out[...] = (dec_in[...] + dot(dmix[...], dwo_v[...])).astype(BF)

    for copy in sends[len(early) :]:
        copy.wait_send()


def local(
    patches,
    visible,
    counts,
    pos_embed,
    mask_token,
    enc_gain,
    enc_qkv,
    enc_wo,
    enc_to_dec,
    dec_gain,
    dec_qkv,
    dec_wo,
):
    vm = pl.BlockSpec(memory_space=pltpu.VMEM)
    sm = pl.BlockSpec(memory_space=pltpu.SMEM)
    hbm = pl.BlockSpec(memory_space=pl.ANY)
    dma = pltpu.SemaphoreType.DMA
    decoded = pl.pallas_call(
        kernel,
        out_shape=jax.ShapeDtypeStruct((TOK, DD), BF),
        in_specs=[hbm, vm, sm, hbm, vm, vm, hbm, hbm, hbm, vm, hbm, hbm],
        out_specs=vm,
        scratch_shapes=[
            pltpu.VMEM((TOK, D), BF),
            pltpu.VMEM((TOK, DD), BF),
            pltpu.VMEM((HA, D), BF),
            pltpu.VMEM((D, DD), BF),
            pltpu.VMEM((DD, 3 * DD), BF),
            pltpu.VMEM((DD, DD), BF),
            pltpu.VMEM((NX, NY, NC, ROWS, WG), BF),
            pltpu.VMEM((NZ, CAP, D), BF),
            pltpu.VMEM((CAP, D), F32),
            pltpu.VMEM((NZ * CAP, HG), BF),
            pltpu.VMEM((3, 4 * CAP, 128), BF),
            pltpu.VMEM((NZ * CAP, 128), F32),
            pltpu.VMEM((HG, D), BF),
            pltpu.VMEM((DD, DD), BF),
            pltpu.VMEM((CAP, HG), BF),
            pltpu.VMEM((CAP, HG), BF),
            pltpu.VMEM((CAP, HG), BF),
            pltpu.VMEM((4, LAYER, DD), BF),
            pltpu.VMEM((TOK, DD), F32),
            pltpu.VMEM((4, 2, 4 * LAYER, 128), BF),
            pltpu.VMEM((2 * LAYER + TOK, DD), BF),
            pltpu.VMEM((DD, 2 * LAYER + TOK), BF),
            pltpu.VMEM((TOK, DD), BF),
            dma((9,)),
            dma((24,)),
            dma((24,)),
            dma((19,)),
            dma((19,)),
            dma((2 * NY,)),
            dma((2 * NY,)),
            dma,
            dma,
            dma((2,)),
            dma((2,)),
        ],
        compiler_params=pltpu.CompilerParams(
            collective_id=0, has_side_effects=True, vmem_limit_bytes=60 * 2**20
        ),
        cost_estimate=pl.CostEstimate(
            flops=3 * 10**9, bytes_accessed=10 * 2**20, transcendentals=3 * 10**6
        ),
        name="volume",
    )(
        patches[0],
        visible[0],
        counts,
        pos_embed,
        mask_token,
        enc_gain,
        enc_qkv,
        enc_wo,
        enc_to_dec,
        dec_gain,
        dec_qkv,
        dec_wo,
    )
    return decoded[None]


def solution(mesh):
    in_specs = (
        P("vol", "seq", None),
        P("vol", "seq", None),
        P("vol", None),
        P("seq", None),
        P(),
        P(),
        P("vol", None),
        P(),
        P(),
        P(),
        P(),
        P(),
    )
    out_specs = P("vol", "seq", None)
    return jax.shard_map(local, mesh=mesh, in_specs=in_specs, out_specs=out_specs, check_vma=False)
```

```python
import functools
import math

import jax
import jax.numpy as jnp
from jax import lax
from jax.experimental import pallas as pl
from jax.experimental.pallas import tpu as pltpu
from jax.sharding import PartitionSpec as P

MESH = pl.DeviceIdType.MESH
BF = jnp.bfloat16
F32 = jnp.float32

HEADS = 12
DHEADS = 16
NX, NY, NC, NZ = 4, 8, 2, 12
CAP = 96
TOK = 256
LAYER = 128
D = 1024
HA = 768
HD = HA // HEADS
HG = HA // 2
WG = 3 * HG
DD = 512
ROWS = 16
HALF = CAP // 2
EPSILON = 1e-06
NEGATIVE = -1e30
OFFSETS = (-3, -2, -1, 0, 1, 2, 3, -4, 4, -5, 5, 6)
OWN = 3
FIRST = 7
SECOND = 11
LOG2E = math.log2(math.e)


def dot(a, b):
    return jnp.dot(a, b, preferred_element_type=F32)


def dot_nt(a, b):
    return lax.dot_general(a, b, (((1,), (1,)), ((), ())), preferred_element_type=F32)


def layer_norm(values, weights):
    centred = values - jnp.mean(values, axis=-1, keepdims=True)
    spread = jnp.mean(centred * centred, axis=-1, keepdims=True)
    return centred * lax.rsqrt(spread + EPSILON) * weights


def slot_r(k):
    return OFFSETS.index(-k) if k < 6 else NZ - 1


def slot_l(k):
    return OFFSETS.index(k)


def kernel(
    patches,
    visible,
    counts,
    pos_embed,
    mask_token,
    enc_gain,
    enc_qkv,
    enc_wo,
    enc_to_dec,
    dec_gain,
    dec_qkv,
    dec_wo,
    out,
    patch_v,
    pos_v,
    wo_v,
    e2d_v,
    dqkv_v,
    dwo_v,
    w_all,
    x_all,
    x_own,
    k_all,
    q_all,
    bias,
    ewv_t,
    dwv_t,
    mix_own,
    mix_send,
    mix_recv,
    dn_all,
    dec_in,
    dq,
    dk,
    dv_t,
    dmix,
    load_sem,
    zs,
    zr,
    ws,
    wr,
    cs,
    cr,
    rs,
    rr,
    hs,
    hr,
):
    v = lax.axis_index("vol")
    z = lax.axis_index("seq")
    core = v % NC
    y = (v // NC) % NY
    x = v // (NC * NY)
    part = z % 2

    def vol_of(px, py, pc):
        return (px * NY + py) * NC + pc

    right = (v, (z + 1) % NZ)
    left = (v, (z + NZ - 1) % NZ)
    mate = (v, z + 1 - 2 * part)
    up = (vol_of(x, (y + 1) % NY, core), z)
    down = (vol_of(x, (y + NY - 1) % NY, core), z)
    sibling = (vol_of(x, y, 1 - core), z)
    x_dev = [(vol_of((x + i) % NX, y, core), z) for i in range(NX)]

    barrier = pltpu.get_barrier_semaphore()
    partners = [right, left, up, down, sibling] + x_dev[1:]
    for device in partners:
        pl.semaphore_signal(barrier, inc=1, device_id=device, device_id_type=MESH)

    loads = {}

    def load(name, src, dst, index):
        copy = pltpu.make_async_copy(src, dst, load_sem.at[index])
        copy.start()
        loads[name] = copy

    for i in range(3):
        column = pl.multiple_of(i * HA + part * HG, 128)
        load(
            "w%d" % i,
            enc_qkv.at[:, pl.ds(column, HG)],
            w_all.at[x, y, core, :, pl.ds(i * HG, HG)],
            i,
        )
    load("patches", patches, patch_v, 3)
    load("pos", pos_embed, pos_v, 4)
    load("wo", enc_wo, wo_v, 5)
    load("e2d", enc_to_dec, e2d_v, 6)
    load("dqkv", dec_qkv, dqkv_v, 7)
    load("dwo", dec_wo, dwo_v, 8)

    sends = []

    def remote(src, dst, send_sem, recv_sem, device):
        copy = pltpu.make_async_remote_copy(
            src_ref=src,
            dst_ref=dst,
            send_sem=send_sem,
            recv_sem=recv_sem,
            device_id=device,
            device_id_type=MESH,
        )
        return copy

    def start(copy):
        copy.start()
        sends.append(copy)

    def z_copy(k, h, to_right):
        rows = pl.ds(h * HALF, HALF)
        slot = slot_r if to_right else slot_l
        side = 0 if to_right else 1
        index = ((k - 1) * 2 + h) * 2 + side
        return remote(
            x_all.at[slot(k - 1), rows],
            x_all.at[slot(k), rows],
            zs.at[index],
            zr.at[index],
            right if to_right else left,
        )

    def z_has(k, h, to_right):
        return k < 6 or (k == 6 and (h == 0) == to_right)

    def z_event(k, h):
        for to_right in (True, False):
            if z_has(k, h, to_right):
                z_copy(k, h, to_right).wait_recv()
                if z_has(k + 1, h, to_right):
                    start(z_copy(k + 1, h, to_right))


    def wx_copy(i, other):
        cell = w_all.at[other, y, core]
        return remote(cell, cell, ws.at[i - 1], wr.at[i - 1], x_dev[i])

    def wy_copy(j, h, upward, step):
        owner = (y + NY - step) % NY if upward else (y + step) % NY
        cell = w_all.at[pl.ds(h * 2, 2), owner, core]
        index = 3 + ((j - 1) * 2 + h) * 2 + (0 if upward else 1)
        return remote(cell, cell, ws.at[index], wr.at[index], up if upward else down)

    def wy_has(j, h, upward):
        return j < 4 or (j == 4 and (h == 0) == upward)

    def wc_copy(offset, of_core):
        cell = w_all.at[:, (y + offset) % NY, of_core]
        return remote(cell, cell, cs.at[offset], cr.at[offset], sibling)

    def wx_event():
        for i in range(1, NX):
            wx_copy(i, (x + NX - i) % NX).wait_recv()
        for h in range(2):
            for upward in (True, False):
                start(wy_copy(1, h, upward, 0))
        start(wc_copy(0, core))

    def wy_event(j, h):
        for upward in (True, False):
            if wy_has(j, h, upward):
                wy_copy(j, h, upward, j).wait_recv()
                if wy_has(j + 1, h, upward):
                    start(wy_copy(j + 1, h, upward, j))
                if h == 1:
                    start(wc_copy(NY - j if upward and j < 4 else j, core))

    def sibling_event():
        for offset in range(NY):
            wc_copy(offset, 1 - core).wait_recv()

    for i in range(3):
        loads["w%d" % i].wait()
    pl.semaphore_wait(barrier, len(partners))
    for i in range(1, NX):
        start(wx_copy(i, x))

    loads["patches"].wait()
    token = lax.broadcasted_iota(jnp.int32, (TOK, CAP), 0)
    slot = lax.broadcasted_iota(jnp.int32, (TOK, CAP), 1)
    chooser = visible[...] == token
    chosen = jnp.where(chooser, 1.0, 0.0)
    x_vis = dot(jnp.transpose(chosen).astype(BF), patch_v[...])
    x_own[...] = x_vis
    normed = layer_norm(x_vis, enc_gain[...].astype(F32)[None]).astype(BF)
    x_all[OWN] = normed
    for h in range(2):
        for to_right in (True, False):
            start(z_copy(1, h, to_right))

    count = counts[0, z]
    live_chosen = jnp.where(chooser & (slot < count), 1.0, 0.0)
    is_visible = jnp.sum(live_chosen, axis=1, keepdims=True) > 0.5

    slot_row = lax.broadcasted_iota(jnp.int32, (CAP, 128), 0)
    for e in range(NZ):
        alive = slot_row < counts[0, (z + OFFSETS[e] + NZ) % NZ]
        bias[e * CAP : (e + 1) * CAP, :] = jnp.where(alive, 0.0, NEGATIVE)
    loads["dqkv"].wait()
    dwv_t[...] = jnp.transpose(dqkv_v[:, 2 * DD :])

    wx_event()
    z_event(1, 0)
    wy_event(1, 0)
    z_event(1, 1)
    wy_event(1, 1)
    z_event(2, 0)
    wy_event(2, 0)
    z_event(2, 1)
    wy_event(2, 1)
    z_event(3, 0)
    wy_event(3, 0)
    z_event(3, 1)
    wy_event(3, 1)
    z_event(4, 0)
    wy_event(4, 0)
    wy_event(4, 1)
    z_event(4, 1)
    sibling_event()
    z_event(5, 0)

    weights = w_all.reshape(D, WG)

    def project_keys(first, last):
        rows = x_all[first:last].reshape((last - first) * CAP, D)
        keys = dot(rows, weights[:, HG : 2 * HG]).astype(BF)
        k_all[first * CAP : last * CAP, :] = keys

    def project_values(first, last):
        rows = x_all[first:last].reshape((last - first) * CAP, D)
        return dot_nt(ewv_t[...], rows).astype(BF)

    lane = lax.broadcasted_iota(jnp.int32, (2 * CAP, 128), 1) // 64

    mate_slot = OWN + 1 - 2 * part
    pair = jnp.concatenate([x_all[mate_slot], x_all[OWN]], axis=0)
    queries = (dot(pair, weights[:, :HG]) * (LOG2E / math.sqrt(HD))).astype(BF)
    for p in range(3):
        two = queries[:, p * 128 : (p + 1) * 128]
        for s in range(2):
            one = jnp.where(lane == s, two, jnp.zeros_like(two))
            q_all[p, s * 2 * CAP : (s + 1) * 2 * CAP, :] = one
    ewv_t[...] = jnp.transpose(weights[:, 2 * HG :])
    project_keys(0, FIRST)

    def attend(p, first, last, values_t):
        cols = slice(p * 128, (p + 1) * 128)
        row_bias = bias[first * CAP : last * CAP, :]
        scores = dot_nt(k_all[first * CAP : last * CAP, cols], q_all[p])
        scores = scores + jnp.concatenate([row_bias] * 3, axis=1)
        top = jnp.max(scores, axis=0, keepdims=True)
        raised = jnp.exp2(scores - top)
        total = jnp.sum(raised, axis=0, keepdims=True)
        return top, total, dot(values_t[cols, :], raised.astype(BF))

    state = {}

    def first_part(p):
        state[p] = attend(p, 0, FIRST, values_first)

    def next_part(p, first, last, values_t):
        old, old_total, old_mixed = state[p]
        top, total, mixed = attend(p, first, last, values_t)
        new = jnp.maximum(old, top)
        a, b = jnp.exp2(old - new), jnp.exp2(top - new)
        state[p] = (new, old_total * a + total * b, old_mixed * a + mixed * b)

    z_event(5, 1)
    values_first = project_values(0, FIRST)
    for p in range(3):
        first_part(p)
    project_keys(FIRST, SECOND)
    values_second = project_values(FIRST, SECOND)
    for p in range(3):
        next_part(p, FIRST, SECOND, values_second)
    z_event(6, 0)
    z_event(6, 1)
    project_keys(SECOND, NZ)
    values_last = project_values(SECOND, NZ)
    early = list(sends)
    back = []
    for p in range(3):
        next_part(p, SECOND, NZ, values_last)
        _, total, mixed = state[p]
        turned = jnp.transpose(mixed / total)
        joined = jnp.where(lane == 0, turned[: 2 * CAP], turned[2 * CAP :]).astype(BF)
        cols = slice(p * 128, (p + 1) * 128)
        mix_send[p] = joined[:CAP]
        mix_own[:, cols] = joined[CAP:]
        back.append(remote(mix_send.at[p], mix_recv.at[p], rs.at[p], rr.at[p], mate))
        back[p].start()

    sends.extend(back)
    loads["wo"].wait()
    own_rows = pl.multiple_of(part * HG, 128)
    mate_rows = pl.multiple_of((1 - part) * HG, 128)
    enc_out = x_own[...] + dot(mix_own[...], wo_v[pl.ds(own_rows, HG), :])
    loads["e2d"].wait()
    loads["pos"].wait()
    loads["dwo"].wait()
    for copy in early:
        copy.wait_send()
    for copy in back:
        copy.wait_recv()
    mix_mate = jnp.concatenate([mix_recv[p] for p in range(3)], axis=1)
    enc_out = enc_out + dot(mix_mate, wo_v[pl.ds(mate_rows, HG), :])
    latent = dot(enc_out.astype(BF), e2d_v[...]).astype(BF)
    placed = dot(live_chosen.astype(BF), latent)
    dec = jnp.where(is_visible, placed, mask_token[...].astype(F32)[None]) + pos_v[...].astype(F32)
    dec_in[...] = dec
    dnorm = layer_norm(dec, dec_gain[...].astype(F32)[None]).astype(BF)
    dn_all[1] = dnorm[:LAYER]
    dn_all[2] = dnorm[LAYER:]
    halo_r = remote(dn_all.at[2], dn_all.at[0], hs.at[0], hr.at[0], right)
    halo_l = remote(dn_all.at[1], dn_all.at[3], hs.at[1], hr.at[1], left)
    start(halo_r)
    start(halo_l)

    scale = LOG2E / math.sqrt(DD // DHEADS)
    proj = (dot(dnorm, dqkv_v[:, :DD]) * scale).astype(BF)
    dk[LAYER : LAYER + TOK, :] = dot(dnorm, dqkv_v[:, DD : 2 * DD]).astype(BF)
    dv_t[:, LAYER : LAYER + TOK] = dot_nt(dwv_t[...], dnorm).astype(BF)
    quad_lane = lax.broadcasted_iota(jnp.int32, (TOK, 128), 1) // 32
    for g in range(4):
        four = proj[:, g * 128 : (g + 1) * 128]
        for s in range(4):
            one = jnp.where(quad_lane == s, four, jnp.zeros_like(four))
            for level in range(2):
                dq[g, level, s * LAYER : (s + 1) * LAYER, :] = one[level * LAYER : (level + 1) * LAYER]

    def quad(g, level, first, last, off_grid):
        scores = dot_nt(dk[first:last, g * 128 : (g + 1) * 128], dq[g, level])
        if off_grid is not None:
            scores = scores + off_grid
        top = jnp.max(scores, axis=0, keepdims=True)
        raised = jnp.exp2(scores - top)
        total = jnp.sum(raised, axis=0, keepdims=True)
        weight = raised.astype(BF)
        wide = dot(dv_t[g * 128 : (g + 1) * 128, first:last], weight)
        mixed = [wide[s * 32 : (s + 1) * 32, s * LAYER : (s + 1) * LAYER] for s in range(4)]
        return top, total, mixed

    inner = {}
    for g in range(4):
        for level in range(2):
            inner[g, level] = quad(g, level, LAYER, LAYER + TOK, None)

    edges = ((0, LAYER), (LAYER + TOK, 2 * LAYER + TOK))
    halo_r.wait_recv()
    halo_l.wait_recv()
    for level, (first, last) in enumerate(edges):
        rows = dn_all[3 * level]
        dk[first:last, :] = dot(rows, dqkv_v[:, DD : 2 * DD]).astype(BF)
        dv_t[:, first:last] = dot_nt(dwv_t[...], rows).astype(BF)
    off = (jnp.where(z == 0, NEGATIVE, 0.0), jnp.where(z == NZ - 1, NEGATIVE, 0.0))
    for g in range(4):
        for level, (first, last) in enumerate(edges):
            old, old_total, old_mixed = inner[g, level]
            top, total, mixed = quad(g, level, first, last, off[level])
            new = jnp.maximum(old, top)
            a, b = jnp.exp2(old - new), jnp.exp2(top - new)
            share = 1.0 / (old_total * a + total * b)
            a, b = a * share, b * share
            heads = []
            for s in range(4):
                at = slice(s * LAYER, (s + 1) * LAYER)
                heads.append(old_mixed[s] * a[:, at] + mixed[s] * b[:, at])
            turned = jnp.transpose(jnp.concatenate(heads, axis=0))
            dmix[level * LAYER : (level + 1) * LAYER, g * 128 : (g + 1) * 128] = turned.astype(BF)
    out[...] = (dec_in[...] + dot(dmix[...], dwo_v[...])).astype(BF)

    for copy in sends[len(early) :]:
        copy.wait_send()


def local(
    patches,
    visible,
    counts,
    pos_embed,
    mask_token,
    enc_gain,
    enc_qkv,
    enc_wo,
    enc_to_dec,
    dec_gain,
    dec_qkv,
    dec_wo,
):
    vm = pl.BlockSpec(memory_space=pltpu.VMEM)
    sm = pl.BlockSpec(memory_space=pltpu.SMEM)
    hbm = pl.BlockSpec(memory_space=pl.ANY)
    dma = pltpu.SemaphoreType.DMA
    decoded = pl.pallas_call(
        kernel,
        out_shape=jax.ShapeDtypeStruct((TOK, DD), BF),
        in_specs=[hbm, vm, sm, hbm, vm, vm, hbm, hbm, hbm, vm, hbm, hbm],
        out_specs=vm,
        scratch_shapes=[
            pltpu.VMEM((TOK, D), BF),
            pltpu.VMEM((TOK, DD), BF),
            pltpu.VMEM((HA, D), BF),
            pltpu.VMEM((D, DD), BF),
            pltpu.VMEM((DD, 3 * DD), BF),
            pltpu.VMEM((DD, DD), BF),
            pltpu.VMEM((NX, NY, NC, ROWS, WG), BF),
            pltpu.VMEM((NZ, CAP, D), BF),
            pltpu.VMEM((CAP, D), F32),
            pltpu.VMEM((NZ * CAP, HG), BF),
            pltpu.VMEM((3, 4 * CAP, 128), BF),
            pltpu.VMEM((NZ * CAP, 128), F32),
            pltpu.VMEM((HG, D), BF),
            pltpu.VMEM((DD, DD), BF),
            pltpu.VMEM((CAP, HG), BF),
            pltpu.VMEM((3, CAP, 128), BF),
            pltpu.VMEM((3, CAP, 128), BF),
            pltpu.VMEM((4, LAYER, DD), BF),
            pltpu.VMEM((TOK, DD), F32),
            pltpu.VMEM((4, 2, 4 * LAYER, 128), BF),
            pltpu.VMEM((2 * LAYER + TOK, DD), BF),
            pltpu.VMEM((DD, 2 * LAYER + TOK), BF),
            pltpu.VMEM((TOK, DD), BF),
            dma((9,)),
            dma((24,)),
            dma((24,)),
            dma((19,)),
            dma((19,)),
            dma((NY,)),
            dma((NY,)),
            dma((3,)),
            dma((3,)),
            dma((2,)),
            dma((2,)),
        ],
        compiler_params=pltpu.CompilerParams(
            collective_id=0, has_side_effects=True, vmem_limit_bytes=60 * 2**20
        ),
        cost_estimate=pl.CostEstimate(
            flops=3 * 10**9, bytes_accessed=10 * 2**20, transcendentals=3 * 10**6
        ),
        name="volume",
    )(
        patches[0],
        visible[0],
        counts,
        pos_embed,
        mask_token,
        enc_gain,
        enc_qkv,
        enc_wo,
        enc_to_dec,
        dec_gain,
        dec_qkv,
        dec_wo,
    )
    return decoded[None]


def solution(mesh):
    in_specs = (
        P("vol", "seq", None),
        P("vol", "seq", None),
        P("vol", None),
        P("seq", None),
        P(),
        P(),
        P("vol", None),
        P(),
        P(),
        P(),
        P(),
        P(),
    )
    out_specs = P("vol", "seq", None)
    return jax.shard_map(local, mesh=mesh, in_specs=in_specs, out_specs=out_specs, check_vma=False)
```
